32 devices in a mesh: scen: 8 (over y, x, core), fs: 4 (over z).
Axes of the slice: x: 2, y: 2, z: 4, core: 2. Of those that a mesh axis runs over, the one named last changes fastest.
Arguments:
- scen_rhs: float32 [64, 64, 64, 128], P('scen', 'fs')
- first_rhs: float32 [4, 4096, 128], P('fs', 'scen'), may hold values from -6 to 6
- diag_blocks: float32 [64, 64, 64, 64], P('scen', 'fs')
- diag_inverse: bfloat16 [64, 64, 64, 64], P('scen', 'fs')
- couplings: float32 [64, 64, 2, 64, 64], P('scen', 'fs'), may hold values from -0.125 to 0.125
- border: float32 [64, 64, 64, 64], P('scen', 'fs'), may hold values from -0.125 to 0.125
- border_block: int32 [64, 64], P('scen', 'fs'), may hold values from 0 to 63
- first_diag: float32 [4, 4096], P('fs', 'scen'), may hold values from 0.5 to 2
- schur_inverse: bfloat16 [4, 4096, 4, 4096], P(None, 'scen', 'fs')
Outputs:
- scen_sol: float32 [64, 64, 64, 128], P('scen', 'fs')
- first_sol: float32 [4, 4096, 128], P('fs', 'scen')
- first_res: float32 [4, 4096, 128], P('fs', 'scen')
The draws below stay inside these ranges and needn't reach their ends.
All inputs are finite; a program needn't handle non-finite values.
Results may differ from the reference program's by a relative error of at most 0.0049.
Values may be sent and summed in bfloat16 or wider, within the bound.
A program may use at most 128 MiB of HBM per device.

```python
import math
import jax
import jax.numpy as jnp
from jax import lax

N0 = 16384
WINDOWS = 64
WIN = 64
R = 128
ROUNDS = 2
SCEN = 64
GROUPS = 4
GROUP_ROWS = 4096
BLOCKS = 64


def scenario_ramp():
    count = max(SCEN - 1, 1)
    return jnp.arange(SCEN, dtype=jnp.float32) / count


def draw_scen_rhs(key, part):
    base = jax.random.fold_in(key, 41)
    shape = (SCEN, WINDOWS, WIN, R)
    ramp = scenario_ramp()
    values = jnp.clip(jax.random.normal(base, shape, jnp.float32), -5.0, 5.0)
    rise = jnp.exp(math.log(4.0) * ramp)
    return values * rise[:, None, None, None]


def window_parts(key):
    base = jax.random.fold_in(key, 17)
    key_scale, key_mix = jax.random.split(base)
    scales = jnp.exp(jax.random.uniform(key_scale, (SCEN, WINDOWS, WIN), jnp.float32, math.log(2.0), math.log(16.0)))
    ramp = scenario_ramp()
    spread = ((0.05 + 0.3 * ramp) / math.sqrt(WIN))[:, None, None, None]
    mixing = jnp.clip(jax.random.normal(key_mix, (SCEN, WINDOWS, WIN, WIN), jnp.float32), -4.0, 4.0) * spread
    return (scales, mixing)


def draw_diag_blocks(key, part):
    scales, mixing = window_parts(key)
    ident = jnp.eye(WIN, dtype=jnp.float32)
    return scales[..., :, None] * (ident + mixing)


def draw_diag_inverse(key, part):
    scales, mixing = window_parts(key)
    ident = jnp.eye(WIN, dtype=jnp.float32)
    return ((ident - mixing) / scales[..., None, :]).astype(jnp.bfloat16)


def draw_schur_inverse(key, part):
    base = jax.random.fold_in(key, 29)
    key_diag, key_off = jax.random.split(base)
    shape = (GROUPS, GROUP_ROWS, GROUPS, GROUP_ROWS)
    spread = 0.08 / math.sqrt(N0)
    off_part = jnp.clip(jax.random.normal(key_off, shape, jnp.float32), -5.0, 5.0) * spread
    diag_vals = jnp.exp(jax.random.uniform(key_diag, (GROUPS, GROUP_ROWS), jnp.float32, math.log(0.15), math.log(0.45)))
    same_group = lax_eq(0, 2, shape)
    same_row = lax_eq(1, 3, shape)
    on_diag = jnp.logical_and(same_group, same_row).astype(jnp.float32)
    return (off_part + on_diag * diag_vals[None, None, :, :]).astype(jnp.bfloat16)


def lax_eq(first_dim, second_dim, shape):
    first_idx = jax.lax.broadcasted_iota(jnp.int32, shape, first_dim)
    second_idx = jax.lax.broadcasted_iota(jnp.int32, shape, second_dim)
    return first_idx == second_idx


def plant(values, rng, least, top_value):
    spot = [jax.random.randint(jax.random.fold_in(rng, axis), (), 0, length) for axis, length in enumerate(values.shape)]
    widest = values.shape.index(max(values.shape))
    next_to = spot[:widest] + [(spot[widest] + 1) % values.shape[widest]] + spot[widest + 1:]
    return values.at[tuple(spot)].set(least).at[tuple(next_to)].set(top_value)


def block_scale(rng, dims, pieces, least, top_value):
    factor_of, own = 1.0, jax.random.fold_in(rng, 6)
    for axis_at, shards_of in pieces:
        steps = jnp.exp(jax.random.uniform(jax.random.fold_in(own, axis_at), (shards_of,), jnp.float32, least / len(pieces), top_value / len(pieces)))
        factor_of = factor_of * jnp.repeat(steps, dims[axis_at] // shards_of).reshape([-1 if axis == axis_at else 1 for axis in range(len(dims))])
    return factor_of


def bell_draw(stream_key, shape, width, limit, pieces=(), kind=jnp.bfloat16):
    values = jax.random.normal(stream_key, shape, jnp.float32) * width
    if len(pieces) > 0:
        values = block_scale(stream_key, shape, pieces, -0.22, 0.18) * values
    return jnp.clip(values, min=-limit, max=limit).astype(kind)


def setup_inputs(seed: int = 0) -> dict:
    seeds = jax.random.split(jax.random.key(seed), 10)
    scen_rhs = draw_scen_rhs(jax.random.fold_in(seeds[9], 71), 0)
    first_rhs = bell_draw(seeds[1], (GROUPS, GROUP_ROWS, R), 1.0, 6.0, ((0, 4), (1, 8)), jnp.float32)
    diag_blocks = draw_diag_blocks(jax.random.fold_in(seeds[9], 71), 0)
    diag_inverse = draw_diag_inverse(jax.random.fold_in(seeds[9], 71), 0)
    couplings = bell_draw(seeds[4], (SCEN, WINDOWS, 2, WIN, WIN), (0.25 * WIN ** -0.5), 0.125, ((0, 8), (1, 4)), jnp.float32)
    border = bell_draw(seeds[5], (SCEN, WINDOWS, WIN, WIN), (0.25 * WIN ** -0.5), 0.125, ((0, 8), (1, 4)), jnp.float32)
    border_block = plant(jax.random.randint(seeds[6], (SCEN, WINDOWS), 0, BLOCKS), jax.random.fold_in(seeds[6], 1), 0, BLOCKS - 1).astype(jnp.int32)
    first_diag = jnp.clip(jnp.exp(math.log(2.0) - 1.3862944 * jax.random.uniform(seeds[7], (GROUPS, GROUP_ROWS), jnp.float32) ** block_scale(seeds[7], (GROUPS, GROUP_ROWS), ((0, 4), (1, 8)), -0.2, 0.2)), 0.5, 2.0)
    schur_inverse = draw_schur_inverse(jax.random.fold_in(seeds[9], 71), 0)
    return {"scen_rhs": scen_rhs, "first_rhs": first_rhs, "diag_blocks": diag_blocks, "diag_inverse": diag_inverse, "couplings": couplings, "border": border, "border_block": border_block, "first_diag": first_diag, "schur_inverse": schur_inverse}


EXACT = lax.Precision.HIGHEST


def tile_product(mats, values):
    return jnp.einsum('swij,swjr->swir', mats, values, precision=EXACT)


def tile_transpose(mats, values):
    return jnp.einsum('swji,swjr->swir', mats, values, precision=EXACT)


def low_product(mats, values):
    return jnp.einsum('swij,swjr->swir', mats, values, preferred_element_type=jnp.float32)


def reference(scen_rhs, first_rhs, diag_blocks, diag_inverse, couplings, border, border_block, first_diag, schur_inverse):
    per_group = WINDOWS // GROUPS
    group_of = jnp.arange(WINDOWS, dtype=jnp.int32) // per_group
    global_block = (group_of[None, :] * BLOCKS + border_block).reshape(-1).astype(jnp.int32)
    block_total = N0 // WIN
    schur_flat = schur_inverse.reshape(N0, N0)
    first_gain = first_diag.reshape(N0, 1)

    def border_gather(values):
        terms = tile_transpose(border, values).reshape(SCEN * WINDOWS, WIN, R)
        summed = jax.ops.segment_sum(terms, global_block, num_segments=block_total)
        return summed.reshape(N0, R)

    def spread(first_vec):
        blocks = first_vec.reshape(block_total, WIN, R)
        return jnp.take(blocks, global_block, axis=0).reshape(SCEN, WINDOWS, WIN, R)

    scen_res = scen_rhs
    first_res = first_rhs.reshape(N0, R)
    scen_sol = jnp.zeros((SCEN, WINDOWS, WIN, R), jnp.float32)
    first_sol = jnp.zeros((N0, R), jnp.float32)
    for round_index in range(ROUNDS):
        guess = low_product(diag_inverse, scen_res.astype(jnp.bfloat16))
        schur_rhs = (first_res + border_gather(guess)).astype(jnp.bfloat16)
        first_step = lax.dot_general(schur_flat, schur_rhs, (((0,), (0,)), ((), ())), preferred_element_type=jnp.float32)
        widened = spread(first_step)
        coupled = tile_product(border, widened)
        lift = coupled.astype(jnp.bfloat16)
        scen_step = guess - low_product(diag_inverse, lift)
        before = jnp.pad(scen_step, ((0, 0), (1, 0), (0, 0), (0, 0)))[:, :-1]
        after = jnp.pad(scen_step, ((0, 0), (0, 1), (0, 0), (0, 0)))[:, 1:]
        image_scen = tile_product(diag_blocks, scen_step) + tile_product(couplings[:, :, 0], before)
        image_scen = image_scen + tile_product(couplings[:, :, 1], after) + coupled
        image_first = first_gain * first_step - border_gather(scen_step)
        along = jnp.sum(scen_res * image_scen, axis=(0, 1, 2)) + jnp.sum(first_res * image_first, axis=0)
        energy = jnp.sum(image_scen * image_scen, axis=(0, 1, 2)) + jnp.sum(image_first * image_first, axis=0)
        step_size = along / (energy + 1e-6)
        scen_sol = scen_sol + step_size * scen_step
        first_sol = first_sol + step_size * first_step
        scen_res = scen_res - step_size * image_scen
        first_res = first_res - step_size * image_first
    return scen_sol, first_sol.reshape(GROUPS, GROUP_ROWS, R), first_res.reshape(GROUPS, GROUP_ROWS, R)
```

```python
import functools

import jax
import jax.numpy as jnp
from jax import lax
from jax.experimental import pallas as pl
from jax.experimental.pallas import tpu as pltpu
from jax.sharding import PartitionSpec as P

ROUNDS = 2
MIB = 1024 * 1024
MESH = pl.DeviceIdType.MESH
F32 = jnp.float32
BF16 = jnp.bfloat16
VMEM = pl.BlockSpec(memory_space=pltpu.VMEM)
ANY = pl.BlockSpec(memory_space=pl.ANY)


def dot(a, b):
    return jnp.dot(a, b, preferred_element_type=F32)


def dot_t(a, b):
    return lax.dot_general(a, b, (((0,), (0,)), ((), ())), preferred_element_type=F32)


def split(x):
    hi = x.astype(BF16)
    return hi, (x - hi.astype(F32)).astype(BF16)


def guess_kernel(update, size, *refs):
    if update:
        blk, res, image, scale, inv, border, res_out, guess, part, acc = refs
    else:
        blk, res, inv, border, guess, part, acc = refs
    s = pl.program_id(0)
    count = res.shape[1]

    @pl.when(s == 0)
    def _():
        acc[...] = jnp.zeros_like(acc)

    guesses = []
    for w in range(count):
        value = res[0, w]
        if update:
            value = value - scale[...] * image[0, w]
            res_out[0, w] = value
        guesses.append(dot(inv[0, w], value.astype(BF16)))
    terms = []
    for w in range(count):
        guess[0, w] = guesses[w]
        terms.append(dot_t(border[0, w].astype(BF16), guesses[w].astype(BF16)))
    for w in range(count):
        rows = pl.ds(pl.multiple_of(blk[s, w] * size, size), size)
        acc[rows, :] += terms[w]

    @pl.when(s == pl.num_programs(0) - 1)
    def _():
        part[...] = acc[...].astype(BF16)


def step_kernel(size, blk, guess, inv, border, group, step, coupled, part):
    s = pl.program_id(0)
    count = guess.shape[1]

    @pl.when(s == 0)
    def _():
        part[...] = jnp.zeros_like(part)

    places, lifted, borders, terms = [], [], [], []
    for w in range(count):
        rows = pl.ds(pl.multiple_of(blk[s, w] * size, size), size)
        places.append(rows)
        first = group[rows, :]
        hi, lo = split(border[0, w])
        borders.append((hi, lo))
        value = dot(hi, first) + dot(lo, first)
        coupled[0, w] = value
        lifted.append(value.astype(BF16))
    for w in range(count):
        value = guess[0, w] - dot(inv[0, w], lifted[w])
        step[0, w] = value
        vh, vl = split(value)
        hi, lo = borders[w]
        left = jnp.concatenate([hi, lo, hi], axis=0)
        right = jnp.concatenate([vh, vh, vl], axis=0)
        terms.append(dot_t(left, right))
    for w in range(count):
        part[places[w], :] += terms[w]


def by_scenario(shape):
    zeros = (0,) * (len(shape) - 1)
    return pl.BlockSpec((1,) + tuple(shape[1:]), lambda s: (s,) + zeros)


def fixed(shape):
    zeros = (0,) * len(shape)
    return pl.BlockSpec(tuple(shape), lambda s: zeros)


SMEM = pl.BlockSpec(memory_space=pltpu.SMEM)


def guess_call(blk, res, inv, border, rows, image=None, scale=None):
    size, width = res.shape[2:]
    update = image is not None
    field = by_scenario(res.shape)
    ops = [blk, res] + ([image, scale] if update else []) + [inv, border]
    specs = [SMEM, field] + ([field, fixed(scale.shape)] if update else [])
    specs += [by_scenario(inv.shape), by_scenario(border.shape)]
    full = jax.ShapeDtypeStruct(res.shape, F32)
    outs = ([full] if update else []) + [full, jax.ShapeDtypeStruct((rows, width), BF16)]
    out_specs = ([field] if update else []) + [field, fixed((rows, width))]
    return pl.pallas_call(
        functools.partial(guess_kernel, update, size),
        grid=(res.shape[0],),
        in_specs=specs,
        out_specs=out_specs,
        out_shape=outs,
        scratch_shapes=[pltpu.VMEM((rows, width), F32)],
        compiler_params=pltpu.CompilerParams(vmem_limit_bytes=40 * MIB),
        name="guess_windows",
    )(*ops)


def step_call(blk, guess, inv, border, group):
    rows, width = group.shape
    field = by_scenario(guess.shape)
    full = jax.ShapeDtypeStruct(guess.shape, F32)
    return pl.pallas_call(
        functools.partial(step_kernel, guess.shape[2]),
        grid=(guess.shape[0],),
        in_specs=[SMEM, field, by_scenario(inv.shape), by_scenario(border.shape), fixed(group.shape)],
        out_specs=[field, field, fixed((rows, width))],
        out_shape=[full, full, jax.ShapeDtypeStruct((rows, width), F32)],
        compiler_params=pltpu.CompilerParams(vmem_limit_bytes=40 * MIB),
        name="step_windows",
    )(blk, guess, inv, border, group)


def greet(n_s, n_f):
    me_s, me_f = lax.axis_index("scen"), lax.axis_index("fs")
    barrier = pltpu.get_barrier_semaphore()
    for k in range(1, n_s):
        peer = lax.rem(me_s + k, n_s)
        pl.semaphore_signal(barrier, inc=1, device_id=(peer, me_f), device_id_type=MESH)
    for k in range(1, n_f):
        peer = lax.rem(me_f + k, n_f)
        pl.semaphore_signal(barrier, inc=1, device_id=(me_s, peer), device_id_type=MESH)
    pl.semaphore_wait(barrier, n_s + n_f - 2)


def remote(src, dst, send, recv, device):
    return pltpu.make_async_remote_copy(
        src_ref=src, dst_ref=dst, send_sem=send, recv_sem=recv, device_id=device, device_id_type=MESH
    )


def solve_kernel(
    n_s, n_f, part, first, schur, owned, group,
    mats, arrived, rhs, acc, partial, sums, steps,
    load_sem, send1, recv1, send2, recv2, send3, recv3, send4, recv4,
):
    me_s, me_f = lax.axis_index("scen"), lax.axis_index("fs")
    own = first.shape[0]
    aligned = own % 128 == 0
    loads = [pltpu.make_async_copy(schur.at[g], mats.at[g], load_sem.at[g]) for g in range(n_f)]
    for load in loads:
        load.start()
    greet(n_s, n_f)
    sends = []
    for k in range(1, n_s):
        p = lax.rem(me_s + k, n_s)
        sends.append(remote(part.at[p], arrived.at[k], send1.at[k], recv1.at[k], (p, me_f)))
        sends[-1].start()
    total = first[...] + part[me_s].astype(F32)
    for k in range(1, n_s):
        sends[k - 1].wait_recv()
        total = total + arrived[k].astype(F32)
    rhs[0] = total.T.astype(BF16)
    spread = []
    for k in range(1, n_f):
        f = lax.rem(me_f + k, n_f)
        spread.append(remote(rhs.at[0], rhs.at[k], send2.at[k], recv2.at[k], (me_s, f)))
        spread[-1].start()
    for load in loads:
        load.wait()

    def shift(p, k):
        return remote(partial.at[p], sums.at[k], send3.at[k], recv3.at[k], (p, me_f))

    for k in range(n_f):
        if k > 0:
            spread[k - 1].wait_recv()
        g = lax.rem(me_f - k + n_f, n_f)
        if aligned:

            @pl.loop(0, n_s)
            def _(i, k=k, g=g):
                p = lax.rem(me_s + 1 + i, n_s)
                columns = pl.ds(pl.multiple_of(p * own, 128), own)
                value = dot(rhs[k], mats[g, :, columns])
                if k > 0:
                    value = value + acc[p]
                if k < n_f - 1:
                    acc[p] = value
                else:
                    partial[p] = value.astype(BF16)

                    @pl.when(i < n_s - 1)
                    def _():
                        shift(p, i + 1).start()

        else:
            value = dot(rhs[k], mats[g])
            if k > 0:
                value = value + jnp.concatenate([acc[p] for p in range(n_s)], axis=1)
            for p in range(n_s):
                piece = value[:, p * own : (p + 1) * own]
                if k < n_f - 1:
                    acc[p] = piece
                else:
                    partial[p] = piece.astype(BF16)
    if not aligned:
        for k in range(1, n_s):
            shift(lax.rem(me_s + k, n_s), k).start()
    total = partial[me_s].astype(F32)
    for k in range(1, n_s):
        shift(lax.rem(me_s + k, n_s), k).wait_recv()
        total = total + sums[k].astype(F32)
    rounded = total.T.astype(BF16)
    owned[...] = rounded.astype(F32)
    steps[me_s] = rounded
    around = []
    for k in range(1, n_s):
        p = lax.rem(me_s + k, n_s)
        around.append(remote(steps.at[me_s], steps.at[me_s], send4.at[k], recv4.at[k], (p, me_f)))
        around[-1].start()
    for k in range(1, n_s):
        sender = lax.rem(me_s - k + n_s, n_s)
        remote(steps.at[sender], steps.at[sender], send4.at[k], recv4.at[k], (sender, me_f)).wait_recv()
    group[...] = steps[...]
    for k in range(1, n_s):
        sends[k - 1].wait_send()
        shift(lax.rem(me_s + k, n_s), k).wait_send()
        around[k - 1].wait_send()
    for k in range(1, n_f):
        spread[k - 1].wait_send()


def solve_call(n_s, n_f, part, first, schur):
    own, width = first.shape
    dma = pltpu.SemaphoreType.DMA
    return pl.pallas_call(
        functools.partial(solve_kernel, n_s, n_f),
        in_specs=[VMEM, VMEM, ANY],
        out_specs=[VMEM, VMEM],
        out_shape=[
            jax.ShapeDtypeStruct((own, width), F32),
            jax.ShapeDtypeStruct((n_s, own, width), BF16),
        ],
        scratch_shapes=[
            pltpu.VMEM(schur.shape, BF16),
            pltpu.VMEM((n_s, own, width), BF16),
            pltpu.VMEM((n_f, width, own), BF16),
            pltpu.VMEM((n_s, width, own), F32),
            pltpu.VMEM((n_s, width, own), BF16),
            pltpu.VMEM((n_s, width, own), BF16),
            pltpu.VMEM((n_s, own, width), BF16),
            dma((n_f,)),
            dma((n_s,)), dma((n_s,)),
            dma((n_f,)), dma((n_f,)),
            dma((n_s,)), dma((n_s,)),
            dma((n_s,)), dma((n_s,)),
        ],
        compiler_params=pltpu.CompilerParams(
            collective_id=0, has_side_effects=True, vmem_limit_bytes=48 * MIB
        ),
        name="schur_solve",
    )(part, first, schur)


def fold(x):
    return x.reshape(x.shape[0] // 8, 8, x.shape[1]).sum(axis=0)


def image_kernel(n_s, n_f, exact, *refs):
    part, first, owned, gain, step, res, coupled, diag, pairs = refs[:9]
    refs = refs[9:]
    if exact:
        image, refs = refs[0], refs[1:]
    (
        scale, first_out,
        arrived, halo, v_step, v_res, v_coupled, v_diag, v_pairs, high, low, along, energy, inner, outer,
        load_sem, send1, recv1, halo_send, halo_recv, send2, recv2, send3, recv3,
    ) = refs
    me_s, me_f = lax.axis_index("scen"), lax.axis_index("fs")
    scens, count, size = v_step.shape[:3]

    def loads(s):
        moves = ((step, v_step), (diag, v_diag), (pairs, v_pairs), (coupled, v_coupled), (res, v_res))
        return [
            pltpu.make_async_copy(src.at[s], dst.at[s], load_sem.at[s, j]) for j, (src, dst) in enumerate(moves)
        ]

    for s in range(scens):
        for load in loads(s):
            load.start()
    greet(n_s, n_f)
    before = remote(step.at[:, 0], halo.at[1], halo_send.at[1], halo_recv.at[1], (me_s, lax.rem(me_f + n_f - 1, n_f)))
    after = remote(
        step.at[:, count - 1], halo.at[0], halo_send.at[0], halo_recv.at[0], (me_s, lax.rem(me_f + 1, n_f))
    )

    @pl.when(me_f > 0)
    def _():
        before.start()

    @pl.when(me_f < n_f - 1)
    def _():
        after.start()

    sends = []
    for k in range(1, n_s):
        p = lax.rem(me_s + k, n_s)
        sends.append(remote(part.at[p], arrived.at[k], send1.at[k], recv1.at[k], (p, me_f)))
        sends[-1].start()
    along[...] = jnp.zeros_like(along)
    energy[...] = jnp.zeros_like(energy)

    def windows(s, chosen):
        products = []
        for w in chosen:
            mat = jnp.concatenate([v_pairs[s, w, 0], v_diag[s, w], v_pairs[s, w, 1]], axis=1)
            right = high[s, w * size : (w + 3) * size]
            if exact:
                mh, ml = split(mat)
                value = dot(mh, right) + dot(ml, right) + dot(mh, low[s, w * size : (w + 3) * size])
            else:
                value = dot(mat.astype(BF16), right)
            products.append(value)
        a, e = along[...], energy[...]
        for w, value in zip(chosen, products):
            value = value + v_coupled[s, w]
            if exact:
                image[s, w] = value
            a = a + fold(v_res[s, w] * value)
            e = e + fold(value * value)
        along[...] = a
        energy[...] = e

    def place(s, w, value):
        hi, lo = split(value)
        high[s, w * size : (w + 1) * size] = hi
        if exact:
            low[s, w * size : (w + 1) * size] = lo

    @pl.loop(0, scens)
    def _(s):
        for load in loads(s):
            load.wait()
        for w in range(count):
            place(s, w + 1, v_step[s, w])
        windows(s, range(1, count - 1))

    @pl.when(me_f < n_f - 1)
    def _():
        before.wait_recv()

    @pl.when(me_f > 0)
    def _():
        after.wait_recv()

    @pl.when(me_f == n_f - 1)
    def _():
        halo[1] = jnp.zeros(halo.shape[1:], F32)

    @pl.when(me_f == 0)
    def _():
        halo[0] = jnp.zeros(halo.shape[1:], F32)

    @pl.loop(0, scens)
    def _(s):
        place(s, 0, halo[0, s])
        place(s, count + 1, halo[1, s])
        windows(s, (0, count - 1))

    total = part[me_s]
    for k in range(1, n_s):
        sends[k - 1].wait_recv()
        total = total + arrived[k]
    value = gain[...] * owned[...] - total
    a = along[...] + fold(first[...] * value)
    e = energy[...] + fold(value * value)
    inner[0, 0:8] = a
    inner[0, 8:16] = e
    shares = []
    for k in range(1, n_s):
        p = lax.rem(me_s + k, n_s)
        shares.append(remote(inner.at[0], inner.at[k], send2.at[k], recv2.at[k], (p, me_f)))
        shares[-1].start()
    sums = inner[0]
    for k in range(1, n_s):
        shares[k - 1].wait_recv()
        sums = sums + inner[k]
    outer[0] = sums
    lines = []
    for k in range(1, n_f):
        f = lax.rem(me_f + k, n_f)
        lines.append(remote(outer.at[0], outer.at[k], send3.at[k], recv3.at[k], (me_s, f)))
        lines[-1].start()
    for k in range(1, n_f):
        lines[k - 1].wait_recv()
        sums = sums + outer[k]
    a = jnp.sum(sums[0:8], axis=0, keepdims=True)
    e = jnp.sum(sums[8:16], axis=0, keepdims=True)
    ratio = a / (e + 1e-06)
    scale[...] = ratio
    first_out[...] = first[...] - ratio * value

    @pl.when(me_f > 0)
    def _():
        before.wait_send()

    @pl.when(me_f < n_f - 1)
    def _():
        after.wait_send()

    for k in range(1, n_s):
        sends[k - 1].wait_send()
        shares[k - 1].wait_send()
    for k in range(1, n_f):
        lines[k - 1].wait_send()


def image_call(n_s, n_f, exact, part, first, owned, gain, step, res, coupled, diag, pairs):
    own, width = first.shape
    scens, count, size = step.shape[:3]
    dma = pltpu.SemaphoreType.DMA
    outs = [jax.ShapeDtypeStruct((1, width), F32), jax.ShapeDtypeStruct((own, width), F32)]
    if exact:
        outs = [jax.ShapeDtypeStruct(step.shape, F32)] + outs
    padded = (scens, (count + 2) * size, width)
    return pl.pallas_call(
        functools.partial(image_kernel, n_s, n_f, exact),
        in_specs=[VMEM] * 4 + [ANY] * 5,
        out_specs=[VMEM] * len(outs),
        out_shape=outs,
        scratch_shapes=[
            pltpu.VMEM((n_s, own, width), F32),
            pltpu.VMEM((2, scens, size, width), F32),
            pltpu.VMEM(step.shape, F32),
            pltpu.VMEM(res.shape, F32),
            pltpu.VMEM(coupled.shape, F32),
            pltpu.VMEM(diag.shape, F32),
            pltpu.VMEM(pairs.shape, F32),
            pltpu.VMEM(padded, BF16),
            pltpu.VMEM(padded if exact else (1, 16, width), BF16),
            pltpu.VMEM((8, width), F32),
            pltpu.VMEM((8, width), F32),
            pltpu.VMEM((n_s, 16, width), F32),
            pltpu.VMEM((n_f, 16, width), F32),
            dma((scens, 5)),
            dma((n_s,)), dma((n_s,)),
            dma((2,)), dma((2,)),
            dma((n_s,)), dma((n_s,)),
            dma((n_f,)), dma((n_f,)),
        ],
        compiler_params=pltpu.CompilerParams(
            collective_id=1 if exact else 2, has_side_effects=True, vmem_limit_bytes=56 * MIB
        ),
        name="image_exact" if exact else "image_sums",
    )(part, first, owned, gain, step, res, coupled, diag, pairs)


def per_device(
    n_s,
    n_f,
    scen_rhs,
    first_rhs,
    diag_blocks,
    diag_inverse,
    couplings,
    border,
    border_block,
    first_diag,
    schur_inverse,
):
    group_rows = schur_inverse.shape[-1]
    own_rows = first_rhs.shape[1]
    width = scen_rhs.shape[-1]
    schur = schur_inverse.reshape(n_f, own_rows, group_rows)
    gain = first_diag.reshape(own_rows, 1)
    scen_res = scen_rhs
    first_res = first_rhs.reshape(own_rows, width)
    image = scale = scen_sol = first_sol = None
    for round_index in range(ROUNDS):
        if round_index == 0:
            guess, part = guess_call(border_block, scen_res, diag_inverse, border, group_rows)
        else:
            scen_res, guess, part = guess_call(
                border_block, scen_res, diag_inverse, border, group_rows, image, scale
            )
        owned, group = solve_call(n_s, n_f, part.reshape(n_s, own_rows, width), first_res, schur)
        step, coupled, part = step_call(
            border_block, guess, diag_inverse, border, group.reshape(group_rows, width)
        )
        last = round_index == ROUNDS - 1
        found = image_call(
            n_s, n_f, not last, part.reshape(n_s, own_rows, width), first_res, owned, gain,
            step, scen_res, coupled, diag_blocks, couplings,
        )
        if not last:
            image = found[0]
        scale, first_res = found[-2:]
        scen_sol = scale * step if scen_sol is None else scen_sol + scale * step
        first_sol = scale * owned if first_sol is None else first_sol + scale * owned
    return (
        scen_sol,
        first_sol.reshape(1, own_rows, width),
        first_res.reshape(1, own_rows, width),
    )


def solution(mesh):
    return jax.shard_map(
        functools.partial(per_device, mesh.shape["scen"], mesh.shape["fs"]),
        mesh=mesh,
        in_specs=(
            P("scen", "fs", None, None),
            P("fs", "scen", None),
            P("scen", "fs", None, None),
            P("scen", "fs", None, None),
            P("scen", "fs", None, None, None),
            P("scen", "fs", None, None),
            P("scen", "fs"),
            P("fs", "scen"),
            P(None, "scen", "fs", None),
        ),
        out_specs=(P("scen", "fs", None, None), P("fs", "scen", None), P("fs", "scen", None)),
        check_vma=False,
    )
```

```python
import functools

import jax
import jax.numpy as jnp
from jax import lax
from jax.experimental import pallas as pl
from jax.experimental.pallas import tpu as pltpu
from jax.sharding import PartitionSpec as P

ROUNDS = 2
LIMIT = 60 * 1024 * 1024
MESH = pl.DeviceIdType.MESH
F32 = jnp.float32
BF16 = jnp.bfloat16
FAR = jnp.bfloat16
VMEM = pl.BlockSpec(memory_space=pltpu.VMEM)
ANY = pl.BlockSpec(memory_space=pl.ANY)


def dot(a, b):
    return jnp.dot(a, b, preferred_element_type=F32)


def dot_t(a, b):
    return lax.dot_general(a, b, (((0,), (0,)), ((), ())), preferred_element_type=F32)


def split(x):
    hi = x.astype(BF16)
    return hi, (x - hi.astype(F32)).astype(BF16)


def guess_kernel(update, size, *refs):
    if update:
        blk, res, image, scale, inv, border, res_out, guess, part, acc = refs
    else:
        blk, res, inv, border, guess, part, acc = refs
    s = pl.program_id(0)
    count = res.shape[1]

    @pl.when(s == 0)
    def _():
        acc[...] = jnp.zeros_like(acc)

    guesses = []
    for w in range(count):
        value = res[0, w]
        if update:
            value = value - scale[...] * image[0, w]
            res_out[0, w] = value
        guesses.append(dot(inv[0, w], value.astype(BF16)))
    terms = []
    for w in range(count):
        guess[0, w] = guesses[w]
        terms.append(dot_t(border[0, w].astype(BF16), guesses[w].astype(BF16)))
    for w in range(count):
        rows = pl.ds(pl.multiple_of(blk[s, w] * size, size), size)
        acc[rows, :] += terms[w]

    @pl.when(s == pl.num_programs(0) - 1)
    def _():
        part[...] = acc[...].astype(BF16)


def step_kernel(size, blk, guess, inv, border, group, step, coupled, part):
    s = pl.program_id(0)
    count = guess.shape[1]

    @pl.when(s == 0)
    def _():
        part[...] = jnp.zeros_like(part)

    places, lifted, borders, terms = [], [], [], []
    for w in range(count):
        rows = pl.ds(pl.multiple_of(blk[s, w] * size, size), size)
        places.append(rows)
        first = group[rows, :]
        hi, lo = split(border[0, w])
        borders.append((hi, lo))
        value = dot(hi, first) + dot(lo, first)
        coupled[0, w] = value
        lifted.append(value.astype(BF16))
    for w in range(count):
        value = guess[0, w] - dot(inv[0, w], lifted[w])
        step[0, w] = value
        vh, vl = split(value)
        hi, lo = borders[w]
        left = jnp.concatenate([hi, lo, hi], axis=0)
        right = jnp.concatenate([vh, vh, vl], axis=0)
        terms.append(dot_t(left, right))
    for w in range(count):
        part[places[w], :] += terms[w]


def by_scenario(shape):
    zeros = (0,) * (len(shape) - 1)
    return pl.BlockSpec((1,) + tuple(shape[1:]), lambda s: (s,) + zeros)


def fixed(shape):
    zeros = (0,) * len(shape)
    return pl.BlockSpec(tuple(shape), lambda s: zeros)


SMEM = pl.BlockSpec(memory_space=pltpu.SMEM)


def guess_call(blk, res, inv, border, rows, image=None, scale=None):
    size, width = res.shape[2:]
    update = image is not None
    field = by_scenario(res.shape)
    ops = [blk, res] + ([image, scale] if update else []) + [inv, border]
    specs = [SMEM, field] + ([field, fixed(scale.shape)] if update else [])
    specs += [by_scenario(inv.shape), by_scenario(border.shape)]
    full = jax.ShapeDtypeStruct(res.shape, F32)
    outs = ([full] if update else []) + [full, jax.ShapeDtypeStruct((rows, width), BF16)]
    out_specs = ([field] if update else []) + [field, fixed((rows, width))]
    return pl.pallas_call(
        functools.partial(guess_kernel, update, size),
        grid=(res.shape[0],),
        in_specs=specs,
        out_specs=out_specs,
        out_shape=outs,
        scratch_shapes=[pltpu.VMEM((rows, width), F32)],
        compiler_params=pltpu.CompilerParams(vmem_limit_bytes=LIMIT),
        name="guess_windows",
    )(*ops)


def step_call(blk, guess, inv, border, group):
    rows, width = group.shape
    field = by_scenario(guess.shape)
    full = jax.ShapeDtypeStruct(guess.shape, F32)
    return pl.pallas_call(
        functools.partial(step_kernel, guess.shape[2]),
        grid=(guess.shape[0],),
        in_specs=[SMEM, field, by_scenario(inv.shape), by_scenario(border.shape), fixed(group.shape)],
        out_specs=[field, field, fixed((rows, width))],
        out_shape=[full, full, jax.ShapeDtypeStruct((rows, width), F32)],
        compiler_params=pltpu.CompilerParams(vmem_limit_bytes=LIMIT),
        name="step_windows",
    )(blk, guess, inv, border, group)


def greet(devices):
    barrier = pltpu.get_barrier_semaphore()
    for device in devices:
        pl.semaphore_signal(barrier, inc=1, device_id=device, device_id_type=MESH)
    pl.semaphore_wait(barrier, len(devices))


def remote(src, dst, send, recv, device):
    return pltpu.make_async_remote_copy(
        src_ref=src, dst_ref=dst, send_sem=send, recv_sem=recv, device_id=device, device_id_type=MESH
    )


class Places:
    def __init__(self, n_s, n_f):
        self.n_s, self.n_f, self.chips = n_s, n_f, n_s // 2
        self.me_s, self.me_f = lax.axis_index("scen"), lax.axis_index("fs")
        self.chip, self.core = self.me_s // 2, self.me_s % 2
        self.sibling = (self.chip * 2 + 1 - self.core, self.me_f)

    def ahead(self, k):
        return lax.rem(self.chip + k, self.chips)

    def behind(self, k):
        return lax.rem(self.chip - k + self.chips, self.chips)

    def peer(self, k):
        return (self.ahead(k) * 2 + self.core, self.me_f)

    def along(self, k):
        return (self.me_s, lax.rem(self.me_f + k, self.n_f))

    def greeted(self):
        near = [self.sibling] + [self.peer(k) for k in range(1, self.chips)]
        return near + [self.along(k) for k in range(1, self.n_f)]


class Scatter:
    def __init__(self, at, part, pair, mixed, arrived, sems):
        self.at, self.part, self.pair, self.mixed, self.arrived = at, part, pair, mixed, arrived
        near_send, near_recv, far_send, far_recv = sems
        self.near = remote(part.at[:, 1 - at.core], pair, near_send.at[0], near_recv.at[0], at.sibling)
        self.far = [
            remote(mixed.at[k], arrived.at[k], far_send.at[k], far_recv.at[k], at.peer(k))
            for k in range(1, at.chips)
        ]

    def mix(self, chip):
        return self.part[chip, self.at.core].astype(F32) + self.pair[chip].astype(F32)

    def pass_on(self):
        self.near.wait_recv()
        for k, far in enumerate(self.far, 1):
            self.mixed[k] = self.mix(self.at.ahead(k)).astype(self.mixed.dtype)
            far.start()

    def total(self):
        value = self.mix(self.at.chip)
        for k, far in enumerate(self.far, 1):
            far.wait_recv()
            value = value + self.arrived[k].astype(F32)
        return value

    def finish(self):
        self.near.wait_send()
        for far in self.far:
            far.wait_send()


def solve_kernel(
    n_s, n_f, part, first, schur, owned, group,
    mats, pair1, mixed1, arrived1, rhs, acc, partial, pair2, mixed2, arrived2, steps,
    load_sem, a1, b1, c1, d1, line_send, line_recv, a2, b2, c2, d2, far_send, far_recv, near_send, near_recv,
):
    at = Places(n_s, n_f)
    me_f, core, chips = at.me_f, at.core, at.chips
    own = first.shape[0]
    aligned = own % 128 == 0
    loads = [pltpu.make_async_copy(schur.at[g], mats.at[g], load_sem.at[g]) for g in range(n_f)]
    for load in loads:
        load.start()
    greet(at.greeted())
    one = Scatter(at, part, pair1, mixed1, arrived1, (a1, b1, c1, d1))
    two = Scatter(at, partial, pair2, mixed2, arrived2, (a2, b2, c2, d2))
    one.near.start()
    one.pass_on()
    rhs[me_f] = (first[...] + one.total()).T.astype(BF16)

    def hop(t, way):
        g = lax.rem(me_f + (t if way else n_f - t), n_f)
        copy = functools.partial(
            remote, rhs.at[g], rhs.at[g], line_send.at[way, t], line_recv.at[way, t + 1], at.along(n_f - 1 if way else 1)
        )
        has = (me_f + t < n_f) if way else (me_f - t >= 0)
        more = (me_f > 0) if way else (me_f < n_f - 1)
        return copy, has, jnp.logical_and(has, more), g

    def send(t):
        for way in range(2):
            copy, has, goes, g = hop(t, way)
            if t > 0:
                arrival = remote(
                    rhs.at[g], rhs.at[g], line_send.at[way, t], line_recv.at[way, t], at.along(1)
                )
                pl.when(has)(arrival.wait_recv)
            if t < n_f - 1:
                pl.when(goes)(lambda copy=copy: copy().start())

    def multiply(g, begin):
        if aligned:

            @pl.loop(0, n_s)
            def _(p):
                columns = pl.ds(pl.multiple_of(p * own, 128), own)
                value = dot(rhs[g], mats[g, :, columns])
                acc[p] = value if begin else acc[p] + value

        else:
            value = dot(rhs[g], mats[g])
            for p in range(n_s):
                piece = value[:, p * own : (p + 1) * own]
                acc[p] = piece if begin else acc[p] + piece

    send(0)
    for load in loads:
        load.wait()
    multiply(me_f, True)
    for t in range(1, n_f):
        send(t)
        for way in range(2):
            _, has, _, g = hop(t, way)
            pl.when(has)(functools.partial(multiply, g, False))
    for q in range(chips):
        partial[q, 1 - core] = acc[2 * q + 1 - core].astype(BF16)
    two.near.start()
    for q in range(chips):
        partial[q, core] = acc[2 * q + core].astype(BF16)
    two.pass_on()
    rounded = two.total().T.astype(BF16)
    steps[at.chip, core] = rounded

    mine = steps.at[at.chip, core]
    across = [remote(mine, mine, far_send.at[k], far_recv.at[k], at.peer(k)) for k in range(1, chips)]
    for copy in across:
        copy.start()
    over = [remote(mine, mine, near_send.at[0], near_recv.at[0], at.sibling)]
    over[0].start()
    owned[...] = rounded.astype(F32)
    for k in range(1, chips):
        spot = steps.at[at.behind(k), core]
        remote(spot, spot, far_send.at[k], far_recv.at[k], at.sibling).wait_recv()
        over.append(remote(spot, spot, near_send.at[k], near_recv.at[k], at.sibling))
        over[-1].start()
    for k in range(chips):
        spot = steps.at[at.behind(k), 1 - core]
        remote(spot, spot, near_send.at[k], near_recv.at[k], at.sibling).wait_recv()
    group[...] = steps[...]
    one.finish()
    two.finish()
    for copy in across + over:
        copy.wait_send()
    for t in range(n_f - 1):
        for way in range(2):
            copy, _, goes, _ = hop(t, way)
            pl.when(goes)(lambda copy=copy: copy().wait_send())


def solve_call(n_s, n_f, part, first, schur):
    own, width = first.shape
    chips = n_s // 2
    dma = pltpu.SemaphoreType.DMA
    return pl.pallas_call(
        functools.partial(solve_kernel, n_s, n_f),
        in_specs=[VMEM, VMEM, ANY],
        out_specs=[VMEM, VMEM],
        out_shape=[
            jax.ShapeDtypeStruct((own, width), F32),
            jax.ShapeDtypeStruct(part.shape, BF16),
        ],
        scratch_shapes=[
            pltpu.VMEM(schur.shape, BF16),
            pltpu.VMEM((chips, own, width), BF16),
            pltpu.VMEM((chips, own, width), BF16),
            pltpu.VMEM((chips, own, width), BF16),
            pltpu.VMEM((n_f, width, own), BF16),
            pltpu.VMEM((n_s, width, own), F32),
            pltpu.VMEM((chips, 2, width, own), BF16),
            pltpu.VMEM((chips, width, own), BF16),
            pltpu.VMEM((chips, width, own), BF16),
            pltpu.VMEM((chips, width, own), BF16),
            pltpu.VMEM(part.shape, BF16),
            dma((n_f,)),
            dma((1,)), dma((1,)), dma((chips,)), dma((chips,)),
            dma((2, n_f)), dma((2, n_f)),
            dma((1,)), dma((1,)), dma((chips,)), dma((chips,)),
            dma((chips,)), dma((chips,)), dma((chips,)), dma((chips,)),
        ],
        compiler_params=pltpu.CompilerParams(
            collective_id=0, has_side_effects=True, vmem_limit_bytes=LIMIT
        ),
        name="schur_solve",
    )(part, first, schur)


def fold(x):
    return x.reshape(x.shape[0] // 8, 8, x.shape[1]).sum(axis=0)


def image_kernel(n_s, n_f, exact, *refs):
    part, first, owned, gain, step, res, coupled, diag, pairs = refs[:9]
    refs = refs[9:]
    if exact:
        image, refs = refs[0], refs[1:]
    (
        scale, first_out,
        pair, mixed, arrived, halo, v_step, v_res, v_coupled, v_diag, v_pairs, high, low, along, energy, inner, outer,
        load_sem, a1, b1, c1, d1, halo_send, halo_recv, send2, recv2, send3, recv3,
    ) = refs
    at = Places(n_s, n_f)
    me_s, me_f = at.me_s, at.me_f
    scens, count, size = v_step.shape[:3]

    def loads(s):
        moves = ((step, v_step), (diag, v_diag), (pairs, v_pairs), (coupled, v_coupled), (res, v_res))
        return [
            pltpu.make_async_copy(src.at[s], dst.at[s], load_sem.at[s, j]) for j, (src, dst) in enumerate(moves)
        ]

    for s in range(scens):
        for load in loads(s):
            load.start()
    others = [(lax.rem(me_s + k, n_s), me_f) for k in range(1, n_s)]
    greet(others + [at.along(k) for k in range(1, n_f)])
    one = Scatter(at, part, pair, mixed, arrived, (a1, b1, c1, d1))
    one.near.start()
    before = remote(step.at[:, 0], halo.at[1], halo_send.at[1], halo_recv.at[1], (me_s, lax.rem(me_f + n_f - 1, n_f)))
    after = remote(
        step.at[:, count - 1], halo.at[0], halo_send.at[0], halo_recv.at[0], (me_s, lax.rem(me_f + 1, n_f))
    )

    @pl.when(me_f > 0)
    def _():
        before.start()

    @pl.when(me_f < n_f - 1)
    def _():
        after.start()

    along[...] = jnp.zeros_like(along)
    energy[...] = jnp.zeros_like(energy)

    def windows(s, chosen):
        products = []
        for w in chosen:
            mat = jnp.concatenate([v_pairs[s, w, 0], v_diag[s, w], v_pairs[s, w, 1]], axis=1)
            right = high[s, w * size : (w + 3) * size]
            if exact:
                mh, ml = split(mat)
                value = dot(mh, right) + dot(ml, right) + dot(mh, low[s, w * size : (w + 3) * size])
            else:
                value = dot(mat.astype(BF16), right)
            products.append(value)
        a, e = along[...], energy[...]
        for w, value in zip(chosen, products):
            value = value + v_coupled[s, w]
            if exact:
                image[s, w] = value
            a = a + fold(v_res[s, w] * value)
            e = e + fold(value * value)
        along[...] = a
        energy[...] = e

    def place(s, w, value):
        hi, lo = split(value)
        high[s, w * size : (w + 1) * size] = hi
        if exact:
            low[s, w * size : (w + 1) * size] = lo

    one.pass_on()

    @pl.loop(0, scens)
    def _(s):
        for load in loads(s):
            load.wait()
        for w in range(count):
            place(s, w + 1, v_step[s, w])
        windows(s, range(1, count - 1))

    @pl.when(me_f < n_f - 1)
    def _():
        before.wait_recv()

    @pl.when(me_f > 0)
    def _():
        after.wait_recv()

    @pl.when(me_f == n_f - 1)
    def _():
        halo[1] = jnp.zeros(halo.shape[1:], F32)

    @pl.when(me_f == 0)
    def _():
        halo[0] = jnp.zeros(halo.shape[1:], F32)

    @pl.loop(0, scens)
    def _(s):
        place(s, 0, halo[0, s])
        place(s, count + 1, halo[1, s])
        windows(s, (0, count - 1))

    value = gain[...] * owned[...] - one.total()
    a = along[...] + fold(first[...] * value)
    e = energy[...] + fold(value * value)
    inner[0, 0:8] = a
    inner[0, 8:16] = e
    shares = []
    for k in range(1, n_s):
        p = lax.rem(me_s + k, n_s)
        shares.append(remote(inner.at[0], inner.at[k], send2.at[k], recv2.at[k], (p, me_f)))
        shares[-1].start()
    sums = inner[0]
    for k in range(1, n_s):
        shares[k - 1].wait_recv()
        sums = sums + inner[k]
    outer[0] = sums
    lines = []
    for k in range(1, n_f):
        f = lax.rem(me_f + k, n_f)
        lines.append(remote(outer.at[0], outer.at[k], send3.at[k], recv3.at[k], (me_s, f)))
        lines[-1].start()
    for k in range(1, n_f):
        lines[k - 1].wait_recv()
        sums = sums + outer[k]
    a = jnp.sum(sums[0:8], axis=0, keepdims=True)
    e = jnp.sum(sums[8:16], axis=0, keepdims=True)
    ratio = a / (e + 1e-06)
    scale[...] = ratio
    first_out[...] = first[...] - ratio * value

    @pl.when(me_f > 0)
    def _():
        before.wait_send()

    @pl.when(me_f < n_f - 1)
    def _():
        after.wait_send()

    for k in range(1, n_s):
        shares[k - 1].wait_send()
    one.finish()
    for k in range(1, n_f):
        lines[k - 1].wait_send()


def image_call(n_s, n_f, exact, part, first, owned, gain, step, res, coupled, diag, pairs):
    own, width = first.shape
    scens, count, size = step.shape[:3]
    chips = n_s // 2
    dma = pltpu.SemaphoreType.DMA
    outs = [jax.ShapeDtypeStruct((1, width), F32), jax.ShapeDtypeStruct((own, width), F32)]
    if exact:
        outs = [jax.ShapeDtypeStruct(step.shape, F32)] + outs
    padded = (scens, (count + 2) * size, width)
    return pl.pallas_call(
        functools.partial(image_kernel, n_s, n_f, exact),
        in_specs=[VMEM] * 4 + [ANY] * 5,
        out_specs=[VMEM] * len(outs),
        out_shape=outs,
        scratch_shapes=[
            pltpu.VMEM((chips, own, width), F32),
            pltpu.VMEM((chips, own, width), FAR),
            pltpu.VMEM((chips, own, width), FAR),
            pltpu.VMEM((2, scens, size, width), F32),
            pltpu.VMEM(step.shape, F32),
            pltpu.VMEM(res.shape, F32),
            pltpu.VMEM(coupled.shape, F32),
            pltpu.VMEM(diag.shape, F32),
            pltpu.VMEM(pairs.shape, F32),
            pltpu.VMEM(padded, BF16),
            pltpu.VMEM(padded if exact else (1, 16, width), BF16),
            pltpu.VMEM((8, width), F32),
            pltpu.VMEM((8, width), F32),
            pltpu.VMEM((n_s, 16, width), F32),
            pltpu.VMEM((n_f, 16, width), F32),
            dma((scens, 5)),
            dma((1,)), dma((1,)), dma((chips,)), dma((chips,)),
            dma((2,)), dma((2,)),
            dma((n_s,)), dma((n_s,)),
            dma((n_f,)), dma((n_f,)),
        ],
        compiler_params=pltpu.CompilerParams(
            collective_id=1 if exact else 2, has_side_effects=True, vmem_limit_bytes=LIMIT
        ),
        name="image_exact" if exact else "image_sums",
    )(part, first, owned, gain, step, res, coupled, diag, pairs)


def per_device(
    n_s,
    n_f,
    scen_rhs,
    first_rhs,
    diag_blocks,
    diag_inverse,
    couplings,
    border,
    border_block,
    first_diag,
    schur_inverse,
):
    group_rows = schur_inverse.shape[-1]
    own_rows = first_rhs.shape[1]
    width = scen_rhs.shape[-1]
    schur = schur_inverse.reshape(n_f, own_rows, group_rows)
    gain = first_diag.reshape(own_rows, 1)
    scen_res = scen_rhs
    first_res = first_rhs.reshape(own_rows, width)
    image = scale = scen_sol = first_sol = None
    for round_index in range(ROUNDS):
        if round_index == 0:
            guess, part = guess_call(border_block, scen_res, diag_inverse, border, group_rows)
        else:
            scen_res, guess, part = guess_call(
                border_block, scen_res, diag_inverse, border, group_rows, image, scale
            )
        owned, group = solve_call(n_s, n_f, part.reshape(n_s // 2, 2, own_rows, width), first_res, schur)
        step, coupled, part = step_call(
            border_block, guess, diag_inverse, border, group.reshape(group_rows, width)
        )
        last = round_index == ROUNDS - 1
        found = image_call(
            n_s, n_f, not last, part.reshape(n_s // 2, 2, own_rows, width), first_res, owned, gain,
            step, scen_res, coupled, diag_blocks, couplings,
        )
        if not last:
            image = found[0]
        scale, first_res = found[-2:]
        scen_sol = scale * step if scen_sol is None else scen_sol + scale * step
        first_sol = scale * owned if first_sol is None else first_sol + scale * owned
    return (
        scen_sol,
        first_sol.reshape(1, own_rows, width),
        first_res.reshape(1, own_rows, width),
    )


def solution(mesh):
    return jax.shard_map(
        functools.partial(per_device, mesh.shape["scen"], mesh.shape["fs"]),
        mesh=mesh,
        in_specs=(
            P("scen", "fs", None, None),
            P("fs", "scen", None),
            P("scen", "fs", None, None),
            P("scen", "fs", None, None),
            P("scen", "fs", None, None, None),
            P("scen", "fs", None, None),
            P("scen", "fs"),
            P("fs", "scen"),
            P(None, "scen", "fs", None),
        ),
        out_specs=(P("scen", "fs", None, None), P("fs", "scen", None), P("fs", "scen", None)),
        check_vma=False,
    )
```

```python
import functools

import jax
import jax.numpy as jnp
from jax import lax
from jax.experimental import pallas as pl
from jax.experimental.pallas import tpu as pltpu
from jax.sharding import PartitionSpec as P

ROUNDS = 2
LIMIT = 60 * 1024 * 1024
MESH = pl.DeviceIdType.MESH
F32 = jnp.float32
BF16 = jnp.bfloat16
FAR = jnp.bfloat16
VMEM = pl.BlockSpec(memory_space=pltpu.VMEM)
ANY = pl.BlockSpec(memory_space=pl.ANY)


def dot(a, b):
    return jnp.dot(a, b, preferred_element_type=F32)


def dot_t(a, b):
    return lax.dot_general(a, b, (((0,), (0,)), ((), ())), preferred_element_type=F32)


def split(x):
    hi = x.astype(BF16)
    return hi, (x - hi.astype(F32)).astype(BF16)


def twice(x):
    return jnp.concatenate([x, x], axis=0)


def halves(x):
    hi, lo = split(x)
    return jnp.concatenate([hi.astype(F32), lo.astype(F32)], axis=1).astype(BF16)


def guess_kernel(update, size, *refs):
    if update:
        blk, res, image, scale, inv, turned, res_out, guess, part, acc = refs
    else:
        blk, res, inv, border, guess, part, plain, turned, acc = refs
    s = pl.program_id(0)
    count = res.shape[1]

    @pl.when(s == 0)
    def _():
        acc[...] = jnp.zeros_like(acc)

    guesses = []
    for w in range(count):
        value = res[0, w]
        if update:
            value = value - scale[...] * image[0, w]
            res_out[0, w] = value
        else:
            plain[0, w] = halves(border[0, w])
            turned[0, w] = halves(border[0, w].T)
        guesses.append(dot(inv[0, w], value.astype(BF16)))
    terms = []
    for w in range(count):
        guess[0, w] = guesses[w]
        terms.append(dot(turned[0, w], twice(guesses[w].astype(BF16))))
    for w in range(count):
        rows = pl.ds(pl.multiple_of(blk[s, w] * size, size), size)
        acc[rows, :] += terms[w]

    @pl.when(s == pl.num_programs(0) - 1)
    def _():
        part[...] = acc[...].astype(BF16)


def step_kernel(size, blk, guess, inv, plain, turned, group, step, coupled, part):
    s = pl.program_id(0)
    count = guess.shape[1]

    @pl.when(s == 0)
    def _():
        part[...] = jnp.zeros_like(part)

    places, lifted, terms = [], [], []
    for w in range(count):
        rows = pl.ds(pl.multiple_of(blk[s, w] * size, size), size)
        places.append(rows)
        value = dot(plain[0, w], twice(group[rows, :]))
        coupled[0, w] = value
        lifted.append(value.astype(BF16))
    for w in range(count):
        value = guess[0, w] - dot(inv[0, w], lifted[w])
        step[0, w] = value
        vh, vl = split(value)
        terms.append(dot(turned[0, w], twice(vh)) + dot(turned[0, w], twice(vl)))
    for w in range(count):
        part[places[w], :] += terms[w]


def by_scenario(shape):
    zeros = (0,) * (len(shape) - 1)
    return pl.BlockSpec((1,) + tuple(shape[1:]), lambda s: (s,) + zeros)


def fixed(shape):
    zeros = (0,) * len(shape)
    return pl.BlockSpec(tuple(shape), lambda s: zeros)


SMEM = pl.BlockSpec(memory_space=pltpu.SMEM)


def guess_call(blk, res, inv, border, rows, image=None, scale=None):
    size, width = res.shape[2:]
    update = image is not None
    field = by_scenario(res.shape)
    ops = [blk, res] + ([image, scale] if update else []) + [inv, border]
    specs = [SMEM, field] + ([field, fixed(scale.shape)] if update else [])
    specs += [by_scenario(inv.shape), by_scenario(border.shape)]
    full = jax.ShapeDtypeStruct(res.shape, F32)
    outs = ([full] if update else []) + [full, jax.ShapeDtypeStruct((rows, width), BF16)]
    out_specs = ([field] if update else []) + [field, fixed((rows, width))]
    if not update:
        pieces = border.shape[:3] + (2 * size,)
        outs += [jax.ShapeDtypeStruct(pieces, BF16)] * 2
        out_specs += [by_scenario(pieces)] * 2
    return pl.pallas_call(
        functools.partial(guess_kernel, update, size),
        grid=(res.shape[0],),
        in_specs=specs,
        out_specs=out_specs,
        out_shape=outs,
        scratch_shapes=[pltpu.VMEM((rows, width), F32)],
        compiler_params=pltpu.CompilerParams(vmem_limit_bytes=LIMIT),
        name="guess_windows",
    )(*ops)


def step_call(blk, guess, inv, plain, turned, group):
    rows, width = group.shape
    field = by_scenario(guess.shape)
    full = jax.ShapeDtypeStruct(guess.shape, F32)
    return pl.pallas_call(
        functools.partial(step_kernel, guess.shape[2]),
        grid=(guess.shape[0],),
        in_specs=[SMEM, field, by_scenario(inv.shape)]
        + [by_scenario(plain.shape)] * 2
        + [fixed(group.shape)],
        out_specs=[field, field, fixed((rows, width))],
        out_shape=[full, full, jax.ShapeDtypeStruct((rows, width), F32)],
        compiler_params=pltpu.CompilerParams(vmem_limit_bytes=LIMIT),
        name="step_windows",
    )(blk, guess, inv, plain, turned, group)


def greet(devices):
    barrier = pltpu.get_barrier_semaphore()
    for device in devices:
        pl.semaphore_signal(barrier, inc=1, device_id=device, device_id_type=MESH)
    pl.semaphore_wait(barrier, len(devices))


def remote(src, dst, send, recv, device):
    return pltpu.make_async_remote_copy(
        src_ref=src, dst_ref=dst, send_sem=send, recv_sem=recv, device_id=device, device_id_type=MESH
    )


class Places:
    def __init__(self, n_s, n_f):
        self.n_s, self.n_f, self.chips = n_s, n_f, n_s // 2
        self.me_s, self.me_f = lax.axis_index("scen"), lax.axis_index("fs")
        self.chip, self.core = self.me_s // 2, self.me_s % 2
        self.sibling = (self.chip * 2 + 1 - self.core, self.me_f)

    def ahead(self, k):
        return lax.rem(self.chip + k, self.chips)

    def behind(self, k):
        return lax.rem(self.chip - k + self.chips, self.chips)

    def peer(self, k):
        return (self.ahead(k) * 2 + self.core, self.me_f)

    def along(self, k):
        return (self.me_s, lax.rem(self.me_f + k, self.n_f))

    def greeted(self):
        near = [self.sibling] + [self.peer(k) for k in range(1, self.chips)]
        return near + [self.along(k) for k in range(1, self.n_f)]


class Scatter:
    def __init__(self, at, part, pair, mixed, arrived, sems):
        self.at, self.part, self.pair, self.mixed, self.arrived = at, part, pair, mixed, arrived
        near_send, near_recv, far_send, far_recv = sems
        self.order = list(range(1, at.chips)) + [0]
        self.near = {
            k: remote(
                part.at[at.ahead(k), 1 - at.core], pair.at[k], near_send.at[k], near_recv.at[k], at.sibling
            )
            for k in self.order
        }
        self.far = [
            remote(mixed.at[k], arrived.at[k], far_send.at[k], far_recv.at[k], at.peer(k))
            for k in range(1, at.chips)
        ]

    def start(self):
        for k in self.order:
            self.near[k].start()

    def mix(self, k):
        self.near[k].wait_recv()
        return self.part[self.at.ahead(k), self.at.core].astype(F32) + self.pair[k].astype(F32)

    def pass_on(self):
        for k, far in enumerate(self.far, 1):
            self.mixed[k] = self.mix(k).astype(self.mixed.dtype)
            far.start()

    def total(self):
        value = self.mix(0)
        for k, far in enumerate(self.far, 1):
            far.wait_recv()
            value = value + self.arrived[k].astype(F32)
        return value

    def finish(self):
        for k in self.order:
            self.near[k].wait_send()
        for far in self.far:
            far.wait_send()


def solve_kernel(
    n_s, n_f, part, first, schur, owned, group,
    mats, pair1, mixed1, arrived1, rhs, acc, partial, pair2, mixed2, arrived2, steps,
    load_sem, a1, b1, c1, d1, line_send, line_recv, a2, b2, c2, d2, far_send, far_recv, near_send, near_recv,
):
    at = Places(n_s, n_f)
    me_f, core, chips = at.me_f, at.core, at.chips
    own = first.shape[0]
    aligned = own % 128 == 0
    loads = [pltpu.make_async_copy(schur.at[g], mats.at[g], load_sem.at[g]) for g in range(n_f)]
    for load in loads:
        load.start()
    greet(at.greeted())
    one = Scatter(at, part, pair1, mixed1, arrived1, (a1, b1, c1, d1))
    two = Scatter(at, partial, pair2, mixed2, arrived2, (a2, b2, c2, d2))
    one.start()
    one.pass_on()
    rhs[me_f] = (first[...] + one.total()).T.astype(BF16)

    def hop(t, way):
        g = lax.rem(me_f + (t if way else n_f - t), n_f)
        copy = functools.partial(
            remote, rhs.at[g], rhs.at[g], line_send.at[way, t], line_recv.at[way, t + 1], at.along(n_f - 1 if way else 1)
        )
        has = (me_f + t < n_f) if way else (me_f - t >= 0)
        more = (me_f > 0) if way else (me_f < n_f - 1)
        return copy, has, jnp.logical_and(has, more), g

    def send(t):
        for way in range(2):
            copy, has, goes, g = hop(t, way)
            if t > 0:
                arrival = remote(
                    rhs.at[g], rhs.at[g], line_send.at[way, t], line_recv.at[way, t], at.along(1)
                )
                pl.when(has)(arrival.wait_recv)
            if t < n_f - 1:
                pl.when(goes)(lambda copy=copy: copy().start())

    def multiply(g, begin):
        if aligned:

            @pl.loop(0, n_s)
            def _(p):
                columns = pl.ds(pl.multiple_of(p * own, 128), own)
                value = dot(rhs[g], mats[g, :, columns])
                acc[p] = value if begin else acc[p] + value

        else:
            value = dot(rhs[g], mats[g])
            for p in range(n_s):
                piece = value[:, p * own : (p + 1) * own]
                acc[p] = piece if begin else acc[p] + piece

    send(0)
    for load in loads:
        load.wait()
    multiply(me_f, True)
    for t in range(1, n_f):
        send(t)
        for way in range(2):
            _, has, _, g = hop(t, way)
            pl.when(has)(functools.partial(multiply, g, False))
    for k in two.order:
        q = at.ahead(k)
        partial[q, 1 - core] = acc[2 * q + 1 - core].astype(BF16)
        two.near[k].start()
    for k in two.order:
        q = at.ahead(k)
        partial[q, core] = acc[2 * q + core].astype(BF16)
    two.pass_on()
    rounded = two.total().T.astype(BF16)
    steps[at.chip, core] = rounded

    mine = steps.at[at.chip, core]
    across = [remote(mine, mine, far_send.at[k], far_recv.at[k], at.peer(k)) for k in range(1, chips)]
    for copy in across:
        copy.start()
    over = [remote(mine, mine, near_send.at[0], near_recv.at[0], at.sibling)]
    over[0].start()
    owned[...] = rounded.astype(F32)
    for k in range(1, chips):
        spot = steps.at[at.behind(k), core]
        remote(spot, spot, far_send.at[k], far_recv.at[k], at.sibling).wait_recv()
        over.append(remote(spot, spot, near_send.at[k], near_recv.at[k], at.sibling))
        over[-1].start()
    for k in range(chips):
        spot = steps.at[at.behind(k), 1 - core]
        remote(spot, spot, near_send.at[k], near_recv.at[k], at.sibling).wait_recv()
    group[...] = steps[...]
    one.finish()
    two.finish()
    for copy in across + over:
        copy.wait_send()
    for t in range(n_f - 1):
        for way in range(2):
            copy, _, goes, _ = hop(t, way)
            pl.when(goes)(lambda copy=copy: copy().wait_send())


def solve_call(n_s, n_f, part, first, schur):
    own, width = first.shape
    chips = n_s // 2
    dma = pltpu.SemaphoreType.DMA
    return pl.pallas_call(
        functools.partial(solve_kernel, n_s, n_f),
        in_specs=[VMEM, VMEM, ANY],
        out_specs=[VMEM, VMEM],
        out_shape=[
            jax.ShapeDtypeStruct((own, width), F32),
            jax.ShapeDtypeStruct(part.shape, BF16),
        ],
        scratch_shapes=[
            pltpu.VMEM(schur.shape, BF16),
            pltpu.VMEM((chips, own, width), BF16),
            pltpu.VMEM((chips, own, width), BF16),
            pltpu.VMEM((chips, own, width), BF16),
            pltpu.VMEM((n_f, width, own), BF16),
            pltpu.VMEM((n_s, width, own), F32),
            pltpu.VMEM((chips, 2, width, own), BF16),
            pltpu.VMEM((chips, width, own), BF16),
            pltpu.VMEM((chips, width, own), BF16),
            pltpu.VMEM((chips, width, own), BF16),
            pltpu.VMEM(part.shape, BF16),
            dma((n_f,)),
            dma((chips,)), dma((chips,)), dma((chips,)), dma((chips,)),
            dma((2, n_f)), dma((2, n_f)),
            dma((chips,)), dma((chips,)), dma((chips,)), dma((chips,)),
            dma((chips,)), dma((chips,)), dma((chips,)), dma((chips,)),
        ],
        compiler_params=pltpu.CompilerParams(
            collective_id=0, has_side_effects=True, vmem_limit_bytes=LIMIT
        ),
        name="schur_solve",
    )(part, first, schur)


def fold(x):
    return x.reshape(x.shape[0] // 8, 8, x.shape[1]).sum(axis=0)


def image_kernel(n_s, n_f, exact, *refs):
    part, first, owned, gain, step, res, coupled, diag, pairs = refs[:9]
    refs = refs[9:]
    if exact:
        image, refs = refs[0], refs[1:]
    (
        scale, first_out,
        pair, mixed, arrived, halo, v_step, v_res, v_coupled, v_diag, v_pairs, high, low, along, energy, inner, outer,
        load_sem, a1, b1, c1, d1, halo_send, halo_recv, send2, recv2, send3, recv3,
    ) = refs
    at = Places(n_s, n_f)
    me_s, me_f = at.me_s, at.me_f
    scens, count, size = v_step.shape[:3]

    def loads(s):
        moves = ((step, v_step), (diag, v_diag), (pairs, v_pairs), (coupled, v_coupled), (res, v_res))
        return [
            pltpu.make_async_copy(src.at[s], dst.at[s], load_sem.at[s, j]) for j, (src, dst) in enumerate(moves)
        ]

    for s in range(scens):
        for load in loads(s):
            load.start()
    others = [(lax.rem(me_s + k, n_s), me_f) for k in range(1, n_s)]
    greet(others + [at.along(k) for k in range(1, n_f)])
    one = Scatter(at, part, pair, mixed, arrived, (a1, b1, c1, d1))
    one.start()
    before = remote(step.at[:, 0], halo.at[1], halo_send.at[1], halo_recv.at[1], (me_s, lax.rem(me_f + n_f - 1, n_f)))
    after = remote(
        step.at[:, count - 1], halo.at[0], halo_send.at[0], halo_recv.at[0], (me_s, lax.rem(me_f + 1, n_f))
    )

    @pl.when(me_f > 0)
    def _():
        before.start()

    @pl.when(me_f < n_f - 1)
    def _():
        after.start()

    along[...] = jnp.zeros_like(along)
    energy[...] = jnp.zeros_like(energy)

    def windows(s, chosen):
        products = []
        for w in chosen:
            mat = jnp.concatenate([v_pairs[s, w, 0], v_diag[s, w], v_pairs[s, w, 1]], axis=1)
            right = high[s, w * size : (w + 3) * size]
            if exact:
                mh, ml = split(mat)
                value = dot(mh, right) + dot(ml, right) + dot(mh, low[s, w * size : (w + 3) * size])
            else:
                value = dot(mat.astype(BF16), right)
            products.append(value)
        a, e = along[...], energy[...]
        for w, value in zip(chosen, products):
            value = value + v_coupled[s, w]
            if exact:
                image[s, w] = value
            a = a + fold(v_res[s, w] * value)
            e = e + fold(value * value)
        along[...] = a
        energy[...] = e

    def place(s, w, value):
        hi, lo = split(value)
        high[s, w * size : (w + 1) * size] = hi
        if exact:
            low[s, w * size : (w + 1) * size] = lo

    one.pass_on()

    @pl.loop(0, scens)
    def _(s):
        for load in loads(s):
            load.wait()
        for w in range(count):
            place(s, w + 1, v_step[s, w])
        windows(s, range(1, count - 1))

    @pl.when(me_f < n_f - 1)
    def _():
        before.wait_recv()

    @pl.when(me_f > 0)
    def _():
        after.wait_recv()

    @pl.when(me_f == n_f - 1)
    def _():
        halo[1] = jnp.zeros(halo.shape[1:], F32)

    @pl.when(me_f == 0)
    def _():
        halo[0] = jnp.zeros(halo.shape[1:], F32)

    @pl.loop(0, scens)
    def _(s):
        place(s, 0, halo[0, s])
        place(s, count + 1, halo[1, s])
        windows(s, (0, count - 1))

    value = gain[...] * owned[...] - one.total()
    a = along[...] + fold(first[...] * value)
    e = energy[...] + fold(value * value)
    inner[0, 0:8] = a
    inner[0, 8:16] = e
    shares = []
    for k in range(1, n_s):
        p = lax.rem(me_s + k, n_s)
        shares.append(remote(inner.at[0], inner.at[k], send2.at[k], recv2.at[k], (p, me_f)))
        shares[-1].start()
    sums = inner[0]
    for k in range(1, n_s):
        shares[k - 1].wait_recv()
        sums = sums + inner[k]
    outer[0] = sums
    lines = []
    for k in range(1, n_f):
        f = lax.rem(me_f + k, n_f)
        lines.append(remote(outer.at[0], outer.at[k], send3.at[k], recv3.at[k], (me_s, f)))
        lines[-1].start()
    for k in range(1, n_f):
        lines[k - 1].wait_recv()
        sums = sums + outer[k]
    a = jnp.sum(sums[0:8], axis=0, keepdims=True)
    e = jnp.sum(sums[8:16], axis=0, keepdims=True)
    ratio = a / (e + 1e-06)
    scale[...] = ratio
    first_out[...] = first[...] - ratio * value

    @pl.when(me_f > 0)
    def _():
        before.wait_send()

    @pl.when(me_f < n_f - 1)
    def _():
        after.wait_send()

    for k in range(1, n_s):
        shares[k - 1].wait_send()
    one.finish()
    for k in range(1, n_f):
        lines[k - 1].wait_send()


def image_call(n_s, n_f, exact, part, first, owned, gain, step, res, coupled, diag, pairs):
    own, width = first.shape
    scens, count, size = step.shape[:3]
    chips = n_s // 2
    dma = pltpu.SemaphoreType.DMA
    outs = [jax.ShapeDtypeStruct((1, width), F32), jax.ShapeDtypeStruct((own, width), F32)]
    if exact:
        outs = [jax.ShapeDtypeStruct(step.shape, F32)] + outs
    padded = (scens, (count + 2) * size, width)
    return pl.pallas_call(
        functools.partial(image_kernel, n_s, n_f, exact),
        in_specs=[VMEM] * 4 + [ANY] * 5,
        out_specs=[VMEM] * len(outs),
        out_shape=outs,
        scratch_shapes=[
            pltpu.VMEM((chips, own, width), F32),
            pltpu.VMEM((chips, own, width), FAR),
            pltpu.VMEM((chips, own, width), FAR),
            pltpu.VMEM((2, scens, size, width), F32),
            pltpu.VMEM(step.shape, F32),
            pltpu.VMEM(res.shape, F32),
            pltpu.VMEM(coupled.shape, F32),
            pltpu.VMEM(diag.shape, F32),
            pltpu.VMEM(pairs.shape, F32),
            pltpu.VMEM(padded, BF16),
            pltpu.VMEM(padded if exact else (1, 16, width), BF16),
            pltpu.VMEM((8, width), F32),
            pltpu.VMEM((8, width), F32),
            pltpu.VMEM((n_s, 16, width), F32),
            pltpu.VMEM((n_f, 16, width), F32),
            dma((scens, 5)),
            dma((chips,)), dma((chips,)), dma((chips,)), dma((chips,)),
            dma((2,)), dma((2,)),
            dma((n_s,)), dma((n_s,)),
            dma((n_f,)), dma((n_f,)),
        ],
        compiler_params=pltpu.CompilerParams(
            collective_id=1 if exact else 2, has_side_effects=True, vmem_limit_bytes=LIMIT
        ),
        name="image_exact" if exact else "image_sums",
    )(part, first, owned, gain, step, res, coupled, diag, pairs)


def per_device(
    n_s,
    n_f,
    scen_rhs,
    first_rhs,
    diag_blocks,
    diag_inverse,
    couplings,
    border,
    border_block,
    first_diag,
    schur_inverse,
):
    group_rows = schur_inverse.shape[-1]
    own_rows = first_rhs.shape[1]
    width = scen_rhs.shape[-1]
    schur = schur_inverse.reshape(n_f, own_rows, group_rows)
    gain = first_diag.reshape(own_rows, 1)
    scen_res = scen_rhs
    first_res = first_rhs.reshape(own_rows, width)
    image = scale = scen_sol = first_sol = None
    for round_index in range(ROUNDS):
        if round_index == 0:
            guess, part, plain, turned = guess_call(border_block, scen_res, diag_inverse, border, group_rows)
        else:
            scen_res, guess, part = guess_call(
                border_block, scen_res, diag_inverse, turned, group_rows, image, scale
            )
        owned, group = solve_call(n_s, n_f, part.reshape(n_s // 2, 2, own_rows, width), first_res, schur)
        step, coupled, part = step_call(
            border_block, guess, diag_inverse, plain, turned, group.reshape(group_rows, width)
        )
        last = round_index == ROUNDS - 1
        found = image_call(
            n_s, n_f, not last, part.reshape(n_s // 2, 2, own_rows, width), first_res, owned, gain,
            step, scen_res, coupled, diag_blocks, couplings,
        )
        if not last:
            image = found[0]
        scale, first_res = found[-2:]
        scen_sol = scale * step if scen_sol is None else scen_sol + scale * step
        first_sol = scale * owned if first_sol is None else first_sol + scale * owned
    return (
        scen_sol,
        first_sol.reshape(1, own_rows, width),
        first_res.reshape(1, own_rows, width),
    )


def solution(mesh):
    return jax.shard_map(
        functools.partial(per_device, mesh.shape["scen"], mesh.shape["fs"]),
        mesh=mesh,
        in_specs=(
            P("scen", "fs", None, None),
            P("fs", "scen", None),
            P("scen", "fs", None, None),
            P("scen", "fs", None, None),
            P("scen", "fs", None, None, None),
            P("scen", "fs", None, None),
            P("scen", "fs"),
            P("fs", "scen"),
            P(None, "scen", "fs", None),
        ),
        out_specs=(P("scen", "fs", None, None), P("fs", "scen", None), P("fs", "scen", None)),
        check_vma=False,
    )
```

```python
import functools

import jax
import jax.numpy as jnp
from jax import lax
from jax.experimental import pallas as pl
from jax.experimental.pallas import tpu as pltpu
from jax.sharding import PartitionSpec as P

ROUNDS = 2
PIECES = 2
LIMIT = 60 * 1024 * 1024
MESH = pl.DeviceIdType.MESH
F32 = jnp.float32
BF16 = jnp.bfloat16
FAR = jnp.bfloat16
VMEM = pl.BlockSpec(memory_space=pltpu.VMEM)
ANY = pl.BlockSpec(memory_space=pl.ANY)


def dot(a, b):
    return jnp.dot(a, b, preferred_element_type=F32)


def dot_t(a, b):
    return lax.dot_general(a, b, (((0,), (0,)), ((), ())), preferred_element_type=F32)


def split(x):
    hi = x.astype(BF16)
    return hi, (x - hi.astype(F32)).astype(BF16)


def twice(x):
    return jnp.concatenate([x, x], axis=0)


def halves(x):
    hi, lo = split(x)
    return jnp.concatenate([hi.astype(F32), lo.astype(F32)], axis=1).astype(BF16)


def guess_kernel(update, size, *refs):
    if update:
        blk, res, image, scale, inv, turned, res_out, guess, part, acc = refs
    else:
        blk, res, inv, border, guess, part, plain, turned, acc = refs
    s = pl.program_id(0)
    count = res.shape[1]

    @pl.when(s == 0)
    def _():
        acc[...] = jnp.zeros_like(acc)

    guesses = []
    for w in range(count):
        value = res[0, w]
        if update:
            value = value - scale[...] * image[0, w]
            res_out[0, w] = value.astype(BF16)
        else:
            plain[0, w] = halves(border[0, w])
            turned[0, w] = halves(border[0, w].T)
        guesses.append(dot(inv[0, w], value.astype(BF16)))
    terms = []
    for w in range(count):
        guess[0, w] = guesses[w]
        terms.append(dot(turned[0, w], twice(guesses[w].astype(BF16))))
    for w in range(count):
        rows = pl.ds(pl.multiple_of(blk[s, w] * size, size), size)
        acc[rows, :] += terms[w]

    @pl.when(s == pl.num_programs(0) - 1)
    def _():
        part[...] = acc[...].astype(BF16)


def step_kernel(size, blk, guess, inv, plain, turned, group, step, coupled, part):
    s = pl.program_id(0)
    count = guess.shape[1]

    @pl.when(s == 0)
    def _():
        part[...] = jnp.zeros_like(part)

    places, lifted, terms = [], [], []
    for w in range(count):
        rows = pl.ds(pl.multiple_of(blk[s, w] * size, size), size)
        places.append(rows)
        value = dot(plain[0, w], twice(group[rows, :]))
        coupled[0, w] = value
        lifted.append(value.astype(BF16))
    for w in range(count):
        value = guess[0, w] - dot(inv[0, w], lifted[w])
        step[0, w] = value
        vh, vl = split(value)
        terms.append(dot(turned[0, w], twice(vh)) + dot(turned[0, w], twice(vl)))
    for w in range(count):
        part[places[w], :] += terms[w]


def by_scenario(shape):
    zeros = (0,) * (len(shape) - 1)
    return pl.BlockSpec((1,) + tuple(shape[1:]), lambda s: (s,) + zeros)


def fixed(shape):
    zeros = (0,) * len(shape)
    return pl.BlockSpec(tuple(shape), lambda s: zeros)


SMEM = pl.BlockSpec(memory_space=pltpu.SMEM)


def guess_call(blk, res, inv, border, rows, image=None, scale=None):
    size, width = res.shape[2:]
    update = image is not None
    field = by_scenario(res.shape)
    ops = [blk, res] + ([image, scale] if update else []) + [inv, border]
    specs = [SMEM, field] + ([field, fixed(scale.shape)] if update else [])
    specs += [by_scenario(inv.shape), by_scenario(border.shape)]
    full = jax.ShapeDtypeStruct(res.shape, F32)
    outs = ([jax.ShapeDtypeStruct(res.shape, BF16)] if update else []) + [full, jax.ShapeDtypeStruct((rows, width), BF16)]
    out_specs = ([field] if update else []) + [field, fixed((rows, width))]
    if not update:
        pieces = border.shape[:3] + (2 * size,)
        outs += [jax.ShapeDtypeStruct(pieces, BF16)] * 2
        out_specs += [by_scenario(pieces)] * 2
    return pl.pallas_call(
        functools.partial(guess_kernel, update, size),
        grid=(res.shape[0],),
        in_specs=specs,
        out_specs=out_specs,
        out_shape=outs,
        scratch_shapes=[pltpu.VMEM((rows, width), F32)],
        compiler_params=pltpu.CompilerParams(vmem_limit_bytes=LIMIT),
        name="guess_windows",
    )(*ops)


def step_call(blk, guess, inv, plain, turned, group):
    rows, width = group.shape
    field = by_scenario(guess.shape)
    full = jax.ShapeDtypeStruct(guess.shape, F32)
    return pl.pallas_call(
        functools.partial(step_kernel, guess.shape[2]),
        grid=(guess.shape[0],),
        in_specs=[SMEM, field, by_scenario(inv.shape)]
        + [by_scenario(plain.shape)] * 2
        + [fixed(group.shape)],
        out_specs=[field, field, fixed((rows, width))],
        out_shape=[full, full, jax.ShapeDtypeStruct((rows, width), F32)],
        compiler_params=pltpu.CompilerParams(vmem_limit_bytes=LIMIT),
        name="step_windows",
    )(blk, guess, inv, plain, turned, group)


def greet(devices):
    barrier = pltpu.get_barrier_semaphore()
    for device in devices:
        pl.semaphore_signal(barrier, inc=1, device_id=device, device_id_type=MESH)
    pl.semaphore_wait(barrier, len(devices))


def remote(src, dst, send, recv, device):
    return pltpu.make_async_remote_copy(
        src_ref=src, dst_ref=dst, send_sem=send, recv_sem=recv, device_id=device, device_id_type=MESH
    )


class Places:
    def __init__(self, n_s, n_f):
        self.n_s, self.n_f, self.chips = n_s, n_f, n_s // 2
        self.me_s, self.me_f = lax.axis_index("scen"), lax.axis_index("fs")
        self.chip, self.core = self.me_s // 2, self.me_s % 2
        self.sibling = (self.chip * 2 + 1 - self.core, self.me_f)

    def ahead(self, k):
        return lax.rem(self.chip + k, self.chips)

    def behind(self, k):
        return lax.rem(self.chip - k + self.chips, self.chips)

    def peer(self, k):
        return (self.ahead(k) * 2 + self.core, self.me_f)

    def along(self, k):
        return (self.me_s, lax.rem(self.me_f + k, self.n_f))

    def greeted(self):
        near = [self.sibling] + [self.peer(k) for k in range(1, self.chips)]
        return near + [self.along(k) for k in range(1, self.n_f)]


class Scatter:
    def __init__(self, at, part, pair, mixed, arrived, sems):
        self.at, self.part, self.pair, self.mixed, self.arrived = at, part, pair, mixed, arrived
        near_send, near_recv, far_send, far_recv = sems
        self.order = list(range(1, at.chips)) + [0]
        self.near = {
            k: remote(
                part.at[at.ahead(k), 1 - at.core], pair.at[k], near_send.at[k], near_recv.at[k], at.sibling
            )
            for k in self.order
        }
        self.far = [
            remote(mixed.at[k], arrived.at[k], far_send.at[k], far_recv.at[k], at.peer(k))
            for k in range(1, at.chips)
        ]

    def start(self):
        for k in self.order:
            self.near[k].start()

    def mix(self, k):
        self.near[k].wait_recv()
        return self.part[self.at.ahead(k), self.at.core].astype(F32) + self.pair[k].astype(F32)

    def pass_on(self):
        for k, far in enumerate(self.far, 1):
            self.mixed[k] = self.mix(k).astype(self.mixed.dtype)
            far.start()

    def total(self):
        value = self.mix(0)
        for k, far in enumerate(self.far, 1):
            far.wait_recv()
            value = value + self.arrived[k].astype(F32)
        return value

    def finish(self):
        for k in self.order:
            self.near[k].wait_send()
        for far in self.far:
            far.wait_send()


def solve_kernel(
    n_s, n_f, part, first, schur, owned, group,
    mats, pair1, mixed1, arrived1, rhs, acc, partial, pair2, mixed2, arrived2, steps,
    load_sem, a1, b1, c1, d1, line_send, line_recv, a2, b2, c2, d2, far_send, far_recv, near_send, near_recv,
):
    at = Places(n_s, n_f)
    me_f, core, chips = at.me_f, at.core, at.chips
    own = first.shape[0]
    aligned = own % 128 == 0
    loads = [pltpu.make_async_copy(schur.at[g], mats.at[g], load_sem.at[g]) for g in range(n_f)]
    for load in loads:
        load.start()
    greet(at.greeted())
    half = own // PIECES
    bands = [pl.ds(h * half, half) for h in range(PIECES)]
    ones = [
        Scatter(
            at, part.at[:, :, bands[h]], pair1.at[h], mixed1.at[h], arrived1.at[h],
            (a1.at[h], b1.at[h], c1.at[h], d1.at[h]),
        )
        for h in range(PIECES)
    ]
    two = Scatter(at, partial, pair2, mixed2, arrived2, (a2, b2, c2, d2))
    for one in ones:
        one.start()
    for one in ones:
        one.pass_on()

    def hop(t, way):
        g = lax.rem(me_f + (t if way else n_f - t), n_f)
        has = (me_f + t < n_f) if way else (me_f - t >= 0)
        more = (me_f > 0) if way else (me_f < n_f - 1)
        return g, has, jnp.logical_and(has, more)

    def moved(h, t, way, later):
        spot = rhs.at[hop(t, way)[0], h]
        to = at.along(n_f - 1 if way else 1)
        return remote(spot, spot, line_send.at[h, way, t], line_recv.at[h, way, t + later], to)

    def send(h, t):
        for way in range(2):
            _, has, goes = hop(t, way)
            if t > 0:
                pl.when(has)(lambda way=way: moved(h, t, way, 0).wait_recv())
            if t < n_f - 1:
                pl.when(goes)(lambda way=way: moved(h, t, way, 1).start())

    def multiply(g, begin):
        if aligned:

            @pl.loop(0, n_s)
            def _(p):
                columns = pl.ds(pl.multiple_of(p * own, 128), own)
                value = dot(rhs[g, 0], mats[g, bands[0], columns])
                for h in range(1, PIECES):
                    value = value + dot(rhs[g, h], mats[g, bands[h], columns])
                acc[p] = value if begin else acc[p] + value

        else:
            value = dot(rhs[g, 0], mats[g, bands[0]])
            for h in range(1, PIECES):
                value = value + dot(rhs[g, h], mats[g, bands[h]])
            for p in range(n_s):
                piece = value[:, p * own : (p + 1) * own]
                acc[p] = piece if begin else acc[p] + piece

    for h, one in enumerate(ones):
        rhs[me_f, h] = (first[bands[h]] + one.total()).T.astype(BF16)
        send(h, 0)
    for load in loads:
        load.wait()
    multiply(me_f, True)
    for t in range(1, n_f):
        for h in range(PIECES):
            send(h, t)
        left, from_left, _ = hop(t, 0)
        right, from_right, _ = hop(t, 1)
        pl.when(from_left)(functools.partial(multiply, left, False))
        alone = jnp.logical_and(from_right, me_f < t)
        pl.when(alone)(functools.partial(multiply, right, False))
    for t in range(1, n_f // 2 + n_f % 2):
        both = jnp.logical_and(hop(t, 0)[1], hop(t, 1)[1])
        pl.when(both)(functools.partial(multiply, hop(t, 1)[0], False))
    for k in two.order:
        q = at.ahead(k)
        partial[q, 1 - core] = acc[2 * q + 1 - core].astype(BF16)
        two.near[k].start()
    for k in two.order:
        q = at.ahead(k)
        partial[q, core] = acc[2 * q + core].astype(BF16)
    two.pass_on()
    rounded = two.total().T.astype(BF16)
    steps[at.chip, core] = rounded

    mine = steps.at[at.chip, core]
    across = [remote(mine, mine, far_send.at[k], far_recv.at[k], at.peer(k)) for k in range(1, chips)]
    for copy in across:
        copy.start()
    over = [remote(mine, mine, near_send.at[0], near_recv.at[0], at.sibling)]
    over[0].start()
    owned[...] = rounded.astype(F32)
    for k in range(1, chips):
        spot = steps.at[at.behind(k), core]
        remote(spot, spot, far_send.at[k], far_recv.at[k], at.sibling).wait_recv()
        over.append(remote(spot, spot, near_send.at[k], near_recv.at[k], at.sibling))
        over[-1].start()
    for k in range(chips):
        spot = steps.at[at.behind(k), 1 - core]
        remote(spot, spot, near_send.at[k], near_recv.at[k], at.sibling).wait_recv()
    group[...] = steps[...]
    for one in ones:
        one.finish()
    two.finish()
    for copy in across + over:
        copy.wait_send()
    for t in range(n_f - 1):
        for way in range(2):
            for h in range(PIECES):
                pl.when(hop(t, way)[2])(lambda h=h, t=t, way=way: moved(h, t, way, 1).wait_send())


def solve_call(n_s, n_f, part, first, schur):
    own, width = first.shape
    chips = n_s // 2
    banded = (PIECES, chips, own // PIECES, width)
    dma = pltpu.SemaphoreType.DMA
    return pl.pallas_call(
        functools.partial(solve_kernel, n_s, n_f),
        in_specs=[VMEM, VMEM, ANY],
        out_specs=[VMEM, VMEM],
        out_shape=[
            jax.ShapeDtypeStruct((own, width), F32),
            jax.ShapeDtypeStruct(part.shape, BF16),
        ],
        scratch_shapes=[
            pltpu.VMEM(schur.shape, BF16),
            pltpu.VMEM(banded, BF16),
            pltpu.VMEM(banded, BF16),
            pltpu.VMEM(banded, BF16),
            pltpu.VMEM((n_f, PIECES, width, own // PIECES), BF16),
            pltpu.VMEM((n_s, width, own), F32),
            pltpu.VMEM((chips, 2, width, own), BF16),
            pltpu.VMEM((chips, width, own), BF16),
            pltpu.VMEM((chips, width, own), BF16),
            pltpu.VMEM((chips, width, own), BF16),
            pltpu.VMEM(part.shape, BF16),
            dma((n_f,)),
            dma((PIECES, chips)), dma((PIECES, chips)), dma((PIECES, chips)), dma((PIECES, chips)),
            dma((PIECES, 2, n_f)), dma((PIECES, 2, n_f)),
            dma((chips,)), dma((chips,)), dma((chips,)), dma((chips,)),
            dma((chips,)), dma((chips,)), dma((chips,)), dma((chips,)),
        ],
        compiler_params=pltpu.CompilerParams(
            collective_id=0, has_side_effects=True, vmem_limit_bytes=LIMIT
        ),
        name="schur_solve",
    )(part, first, schur)


def fold(x):
    return x.reshape(x.shape[0] // 8, 8, x.shape[1]).sum(axis=0)


def image_kernel(n_s, n_f, exact, *refs):
    part, first, owned, gain, step, res, coupled, diag, pairs = refs[:9]
    refs = refs[9:]
    if exact:
        image, refs = refs[0], refs[1:]
    (
        scale, first_out,
        pair, mixed, arrived, halo, v_step, v_res, v_coupled, v_diag, v_pairs, high, low, along, energy, inner, outer,
        load_sem, a1, b1, c1, d1, halo_send, halo_recv, send2, recv2, send3, recv3,
    ) = refs
    at = Places(n_s, n_f)
    me_s, me_f = at.me_s, at.me_f
    scens, count, size = v_step.shape[:3]

    def loads(s):
        moves = ((step, v_step), (diag, v_diag), (pairs, v_pairs), (coupled, v_coupled), (res, v_res))
        return [
            pltpu.make_async_copy(src.at[s], dst.at[s], load_sem.at[s, j]) for j, (src, dst) in enumerate(moves)
        ]

    for s in range(scens):
        for load in loads(s):
            load.start()
    others = [(lax.rem(me_s + k, n_s), me_f) for k in range(1, n_s)]
    greet(others + [at.along(k) for k in range(1, n_f)])
    one = Scatter(at, part, pair, mixed, arrived, (a1, b1, c1, d1))
    one.start()
    before = remote(step.at[:, 0], halo.at[1], halo_send.at[1], halo_recv.at[1], (me_s, lax.rem(me_f + n_f - 1, n_f)))
    after = remote(
        step.at[:, count - 1], halo.at[0], halo_send.at[0], halo_recv.at[0], (me_s, lax.rem(me_f + 1, n_f))
    )

    @pl.when(me_f > 0)
    def _():
        before.start()

    @pl.when(me_f < n_f - 1)
    def _():
        after.start()

    along[...] = jnp.zeros_like(along)
    energy[...] = jnp.zeros_like(energy)

    def windows(s, chosen):
        products = []
        for w in chosen:
            mat = jnp.concatenate([v_pairs[s, w, 0], v_diag[s, w], v_pairs[s, w, 1]], axis=1)
            right = high[s, w * size : (w + 3) * size]
            if exact:
                mh, ml = split(mat)
                value = dot(mh, right) + dot(ml, right) + dot(mh, low[s, w * size : (w + 3) * size])
            else:
                value = dot(mat.astype(BF16), right)
            products.append(value)
        a, e = along[...], energy[...]
        for w, value in zip(chosen, products):
            value = value + v_coupled[s, w]
            if exact:
                image[s, w] = value
            a = a + fold(v_res[s, w].astype(F32) * value)
            e = e + fold(value * value)
        along[...] = a
        energy[...] = e

    def place(s, w, value):
        hi, lo = split(value)
        high[s, w * size : (w + 1) * size] = hi
        if exact:
            low[s, w * size : (w + 1) * size] = lo

    one.pass_on()

    @pl.loop(0, scens)
    def _(s):
        for load in loads(s):
            load.wait()
        for w in range(count):
            place(s, w + 1, v_step[s, w])
        windows(s, range(1, count - 1))

    @pl.when(me_f < n_f - 1)
    def _():
        before.wait_recv()

    @pl.when(me_f > 0)
    def _():
        after.wait_recv()

    @pl.when(me_f == n_f - 1)
    def _():
        halo[1] = jnp.zeros(halo.shape[1:], F32)

    @pl.when(me_f == 0)
    def _():
        halo[0] = jnp.zeros(halo.shape[1:], F32)

    @pl.loop(0, scens)
    def _(s):
        place(s, 0, halo[0, s])
        place(s, count + 1, halo[1, s])
        windows(s, (0, count - 1))

    value = gain[...] * owned[...] - one.total()
    a = along[...] + fold(first[...] * value)
    e = energy[...] + fold(value * value)
    inner[0, 0:8] = a
    inner[0, 8:16] = e
    shares = []
    for k in range(1, n_s):
        p = lax.rem(me_s + k, n_s)
        shares.append(remote(inner.at[0], inner.at[k], send2.at[k], recv2.at[k], (p, me_f)))
        shares[-1].start()
    sums = inner[0]
    for k in range(1, n_s):
        shares[k - 1].wait_recv()
        sums = sums + inner[k]
    outer[0] = sums
    lines = []
    for k in range(1, n_f):
        f = lax.rem(me_f + k, n_f)
        lines.append(remote(outer.at[0], outer.at[k], send3.at[k], recv3.at[k], (me_s, f)))
        lines[-1].start()
    for k in range(1, n_f):
        lines[k - 1].wait_recv()
        sums = sums + outer[k]
    a = jnp.sum(sums[0:8], axis=0, keepdims=True)
    e = jnp.sum(sums[8:16], axis=0, keepdims=True)
    ratio = a / (e + 1e-06)
    scale[...] = ratio
    first_out[...] = first[...] - ratio * value

    @pl.when(me_f > 0)
    def _():
        before.wait_send()

    @pl.when(me_f < n_f - 1)
    def _():
        after.wait_send()

    for k in range(1, n_s):
        shares[k - 1].wait_send()
    one.finish()
    for k in range(1, n_f):
        lines[k - 1].wait_send()


def image_call(n_s, n_f, exact, part, first, owned, gain, step, res, coupled, diag, pairs):
    own, width = first.shape
    scens, count, size = step.shape[:3]
    chips = n_s // 2
    dma = pltpu.SemaphoreType.DMA
    outs = [jax.ShapeDtypeStruct((1, width), F32), jax.ShapeDtypeStruct((own, width), F32)]
    if exact:
        outs = [jax.ShapeDtypeStruct(step.shape, F32)] + outs
    padded = (scens, (count + 2) * size, width)
    return pl.pallas_call(
        functools.partial(image_kernel, n_s, n_f, exact),
        in_specs=[VMEM] * 4 + [ANY] * 5,
        out_specs=[VMEM] * len(outs),
        out_shape=outs,
        scratch_shapes=[
            pltpu.VMEM((chips, own, width), F32),
            pltpu.VMEM((chips, own, width), FAR),
            pltpu.VMEM((chips, own, width), FAR),
            pltpu.VMEM((2, scens, size, width), F32),
            pltpu.VMEM(step.shape, F32),
            pltpu.VMEM(res.shape, res.dtype),
            pltpu.VMEM(coupled.shape, F32),
            pltpu.VMEM(diag.shape, F32),
            pltpu.VMEM(pairs.shape, F32),
            pltpu.VMEM(padded, BF16),
            pltpu.VMEM(padded if exact else (1, 16, width), BF16),
            pltpu.VMEM((8, width), F32),
            pltpu.VMEM((8, width), F32),
            pltpu.VMEM((n_s, 16, width), F32),
            pltpu.VMEM((n_f, 16, width), F32),
            dma((scens, 5)),
            dma((chips,)), dma((chips,)), dma((chips,)), dma((chips,)),
            dma((2,)), dma((2,)),
            dma((n_s,)), dma((n_s,)),
            dma((n_f,)), dma((n_f,)),
        ],
        compiler_params=pltpu.CompilerParams(
            collective_id=1 if exact else 2, has_side_effects=True, vmem_limit_bytes=LIMIT
        ),
        name="image_exact" if exact else "image_sums",
    )(part, first, owned, gain, step, res, coupled, diag, pairs)


def per_device(
    n_s,
    n_f,
    scen_rhs,
    first_rhs,
    diag_blocks,
    diag_inverse,
    couplings,
    border,
    border_block,
    first_diag,
    schur_inverse,
):
    group_rows = schur_inverse.shape[-1]
    own_rows = first_rhs.shape[1]
    width = scen_rhs.shape[-1]
    schur = schur_inverse.reshape(n_f, own_rows, group_rows)
    gain = first_diag.reshape(own_rows, 1)
    scen_res = scen_rhs
    first_res = first_rhs.reshape(own_rows, width)
    image = scale = scen_sol = first_sol = None
    for round_index in range(ROUNDS):
        if round_index == 0:
            guess, part, plain, turned = guess_call(border_block, scen_res, diag_inverse, border, group_rows)
        else:
            scen_res, guess, part = guess_call(
                border_block, scen_res, diag_inverse, turned, group_rows, image, scale
            )
        owned, group = solve_call(n_s, n_f, part.reshape(n_s // 2, 2, own_rows, width), first_res, schur)
        step, coupled, part = step_call(
            border_block, guess, diag_inverse, plain, turned, group.reshape(group_rows, width)
        )
        last = round_index == ROUNDS - 1
        found = image_call(
            n_s, n_f, not last, part.reshape(n_s // 2, 2, own_rows, width), first_res, owned, gain,
            step, scen_res, coupled, diag_blocks, couplings,
        )
        if not last:
            image = found[0]
        scale, first_res = found[-2:]
        scen_sol = scale * step if scen_sol is None else scen_sol + scale * step
        first_sol = scale * owned if first_sol is None else first_sol + scale * owned
    return (
        scen_sol,
        first_sol.reshape(1, own_rows, width),
        first_res.reshape(1, own_rows, width),
    )


def solution(mesh):
    return jax.shard_map(
        functools.partial(per_device, mesh.shape["scen"], mesh.shape["fs"]),
        mesh=mesh,
        in_specs=(
            P("scen", "fs", None, None),
            P("fs", "scen", None),
            P("scen", "fs", None, None),
            P("scen", "fs", None, None),
            P("scen", "fs", None, None, None),
            P("scen", "fs", None, None),
            P("scen", "fs"),
            P("fs", "scen"),
            P(None, "scen", "fs", None),
        ),
        out_specs=(P("scen", "fs", None, None), P("fs", "scen", None), P("fs", "scen", None)),
        check_vma=False,
    )
```
